32 devices in a mesh: groups: 2 (over y), wake: 4 (over x, core), panel: 4 (over z).
Axes of the slice: x: 2, y: 2, z: 4, core: 2. Of those that a mesh axis runs over, the one named last changes fastest.
Arguments:
- positions: float32 [3, 4096], P(None, ('groups', 'wake', 'panel')), parts along dimension 1, may hold values from -1 to 1
- strengths: float32 [3, 4096], P(None, ('groups', 'wake', 'panel')), parts along dimension 1, may hold values from -0.24 to 0.24
- cores: float32 [1, 4096], P(None, ('groups', 'wake', 'panel')), parts along dimension 1, may hold values from 0.05 to 0.2
- panel_centers: float32 [3, 32768], P(None, ('groups', 'wake', 'panel')), parts along dimension 1, may hold values from -1 to 1
- panel_normals: float32 [3, 32768], P(None, ('groups', 'wake', 'panel')), parts along dimension 1, may hold values from -1 to 1, as said below
- panel_areas: float32 [1, 32768], P(None, ('groups', 'wake', 'panel')), parts along dimension 1, may hold values from 0.004 to 0.04
- influence: float32 [32768, 16384], P(('groups', 'wake'), 'panel'), parts along dimension 0, may hold values from -1 to 2.5
- blade_ids: int32 [32768], P(('groups', 'wake', 'panel')), parts along dimension 0, may hold values from 0 to 3
- blade_velocity: float32 [8, 3], P('groups'), parts along dimension 0, may hold values from -4 to 4
Outputs:
- velocity: float32 [3, 4096], P(None, ('groups', 'wake', 'panel')), parts along dimension 1
- stretching: float32 [3, 4096], P(None, ('groups', 'wake', 'panel')), parts along dimension 1
- panel_strengths: float32 [32768], P(('groups', 'wake', 'panel')), parts along dimension 0
The draws below stay inside these ranges and needn't reach their ends.
There are 2 independent parts, one for each index of `groups`. The reference program is written for one: setup_inputs(seed, part) draws one part's arguments, and reference() takes and returns one part's arrays. A program takes and returns all parts, laid end to end along the dimension named above; each array names one. Nothing has to cross between parts.
Inputs may be any that keep to these rules, and one draw needn't show every extreme that they name: `panel_normals`: each column has unit length.
All inputs are finite; a program needn't handle non-finite values.
Results may differ from the reference program's by a relative error of at most 0.0003.
Values sent between devices are 32-bit elements; how exact they have to be, the bound alone decides.
A program may use at most 128 MiB of HBM per device.

```python
import math
import jax
import jax.numpy as jnp
from jax import lax

NP = 16384
BLADES = 4
ITERS = 4
NPART = 2048


def draw_panel_normals(key, part):
    first, second = jax.random.split(jax.random.fold_in(key, 11))
    height = jax.random.uniform(first, (NP,), jnp.float32, -1.0, 1.0)
    turning = jax.random.uniform(second, (NP,), jnp.float32, -math.pi, math.pi)
    radius = jnp.sqrt(jnp.maximum(1.0 - height * height, 0.0))
    return jnp.stack([radius * jnp.cos(turning), radius * jnp.sin(turning), height])


def draw_influence(key, part):
    first, second = jax.random.split(jax.random.fold_in(key, 23))
    spread = jnp.clip(jax.random.normal(first, (NP, NP), jnp.float32), -6.0, 6.0) * (0.5 / math.sqrt(NP))
    diagonal = jax.random.uniform(second, (NP,), jnp.float32, 1.5, 2.5)
    indices = jnp.arange(NP, dtype=jnp.int32)
    return spread.at[indices, indices].set(diagonal)


def set_ends(entries, stream_key, smallest, high):
    place = [jax.random.randint(jax.random.fold_in(stream_key, axis), (), 0, length) for axis, length in enumerate(entries.shape)]
    widest = entries.shape.index(max(entries.shape))
    neighbour = place[:widest] + [(place[widest] + 1) % entries.shape[widest]] + place[widest + 1:]
    return entries.at[tuple(place)].set(smallest).at[tuple(neighbour)].set(high)


def block_scale(rng, extent, cuts, low, largest):
    level = 1.0
    for position, parts in cuts:
        heights = jax.random.uniform(jax.random.fold_in(jax.random.fold_in(rng, 6), position), (parts,), jnp.float32, low / len(cuts), largest / len(cuts))
        level = level * jnp.repeat(jnp.exp(heights), extent[position] // parts).reshape((-1,) + (1,) * (len(extent) - 1 - position))
    return level


def bell_draw(own_key, shape, width, reach, cuts=(), kind=jnp.bfloat16):
    result = jax.random.normal(own_key, shape, jnp.float32) * width
    if len(cuts) > 0:
        result = block_scale(own_key, shape, cuts, -0.22, 0.18) * result
    return jnp.clip(result, min=-reach, max=reach).astype(kind)


def setup_inputs(seed: int = 0, part: int = 0) -> dict:
    keys = jax.random.split(jax.random.key(seed), 10)
    own_keys = jax.random.split(jax.random.fold_in(keys[9], part), 10)
    return {
        "positions": jnp.clip(jax.random.uniform(own_keys[0], (3, NPART), jnp.float32, -1.0, 1.0) * block_scale(own_keys[0], (3, NPART), ((1, 16),), -0.4, 0.0), -1.0, 1.0),
        "strengths": bell_draw(own_keys[1], (3, NPART), 0.04, 0.24, ((1, 16),), jnp.float32),
        "cores": jnp.clip(jnp.exp(math.log(0.2) - 1.3862944 * jax.random.uniform(own_keys[2], (1, NPART), jnp.float32) ** block_scale(own_keys[2], (1, NPART), ((1, 16),), -0.2, 0.2)), 0.05, 0.2),
        "panel_centers": jnp.clip(jax.random.uniform(own_keys[3], (3, NP), jnp.float32, -1.0, 1.0) * block_scale(own_keys[3], (3, NP), ((1, 16),), -0.4, 0.0), -1.0, 1.0),
        "panel_normals": draw_panel_normals(jax.random.fold_in(jax.random.fold_in(keys[9], part), 71), part),
        "panel_areas": jnp.clip(jnp.exp(math.log(0.04) - 2.30258502 * jax.random.uniform(own_keys[5], (1, NP), jnp.float32) ** block_scale(own_keys[5], (1, NP), ((1, 16),), -0.2, 0.2)), 0.004, 0.04),
        "influence": draw_influence(jax.random.fold_in(jax.random.fold_in(keys[9], part), 71), part),
        "blade_ids": set_ends(jax.random.randint(own_keys[7], (NP,), 0, BLADES), jax.random.fold_in(own_keys[7], 1), 0, BLADES - 1).astype(jnp.int32),
        "blade_velocity": bell_draw(own_keys[8], (BLADES, 3), 1.0, 4.0, (), jnp.float32),
    }


inv_four_pi = 1.0 / (4.0 * math.pi)
relax_factor = 0.5
freestream = (0.0, 0.0, -1.0)

def vortex_terms(targets, sources):
    target_pos, target_str, target_core = targets
    source_pos, source_str, source_core = sources
    offset_x = target_pos[0][:, None] - source_pos[0][None, :]
    offset_y = target_pos[1][:, None] - source_pos[1][None, :]
    offset_z = target_pos[2][:, None] - source_pos[2][None, :]
    core_sq = 0.5 * (target_core[0][:, None] * target_core[0][:, None] + source_core[0][None, :] * source_core[0][None, :])
    distance = offset_x * offset_x + offset_y * offset_y + offset_z * offset_z + core_sq
    inverse = lax.rsqrt(distance)
    falloff = inverse * inverse * inverse
    steeper = falloff * inverse * inverse
    source_x = source_str[0][None, :]
    source_y = source_str[1][None, :]
    source_z = source_str[2][None, :]
    target_x = target_str[0][:, None]
    target_y = target_str[1][:, None]
    target_z = target_str[2][:, None]
    cross_x = offset_y * source_z - offset_z * source_y
    cross_y = offset_z * source_x - offset_x * source_z
    cross_z = offset_x * source_y - offset_y * source_x
    twist_x = target_y * source_z - target_z * source_y
    twist_y = target_z * source_x - target_x * source_z
    twist_z = target_x * source_y - target_y * source_x
    along = 3.0 * steeper * (target_x * offset_x + target_y * offset_y + target_z * offset_z)
    return jnp.stack([lax.optimization_barrier(jnp.sum(falloff * cross_x, axis=1)), lax.optimization_barrier(jnp.sum(falloff * cross_y, axis=1)), lax.optimization_barrier(jnp.sum(falloff * cross_z, axis=1)), lax.optimization_barrier(jnp.sum(falloff * twist_x - along * cross_x, axis=1)), lax.optimization_barrier(jnp.sum(falloff * twist_y - along * cross_y, axis=1)), lax.optimization_barrier(jnp.sum(falloff * twist_z - along * cross_z, axis=1))])

def wake_terms(targets, sources):
    points = targets[0]
    source_pos, source_str, source_core = sources
    offset_x = points[0][:, None] - source_pos[0][None, :]
    offset_y = points[1][:, None] - source_pos[1][None, :]
    offset_z = points[2][:, None] - source_pos[2][None, :]
    distance = offset_x * offset_x + offset_y * offset_y + offset_z * offset_z + source_core[0][None, :] * source_core[0][None, :]
    inverse = lax.rsqrt(distance)
    falloff = inverse * inverse * inverse
    source_x = source_str[0][None, :]
    source_y = source_str[1][None, :]
    source_z = source_str[2][None, :]
    return jnp.stack([lax.optimization_barrier(jnp.sum(falloff * (offset_y * source_z - offset_z * source_y), axis=1)), lax.optimization_barrier(jnp.sum(falloff * (offset_z * source_x - offset_x * source_z), axis=1)), lax.optimization_barrier(jnp.sum(falloff * (offset_x * source_y - offset_y * source_x), axis=1))])

def panel_terms(targets, sources):
    points = targets[0]
    centers, weights, areas = sources
    offset_x = points[0][:, None] - centers[0][None, :]
    offset_y = points[1][:, None] - centers[1][None, :]
    offset_z = points[2][:, None] - centers[2][None, :]
    distance = offset_x * offset_x + offset_y * offset_y + offset_z * offset_z + 4.0 * areas[0][None, :]
    inverse = lax.rsqrt(distance)
    weighted = weights[0][None, :] * inverse * inverse * inverse
    return jnp.stack([lax.optimization_barrier(jnp.sum(weighted * offset_x, axis=1)), lax.optimization_barrier(jnp.sum(weighted * offset_y, axis=1)), lax.optimization_barrier(jnp.sum(weighted * offset_z, axis=1))])

def tiles(array):
    return jnp.moveaxis(array.reshape(array.shape[0], -1, 128), 1, 0)

def untile(array):
    return jnp.moveaxis(array, 0, 1).reshape(array.shape[1], -1)

def reference(positions, strengths, cores, panel_centers, panel_normals, panel_areas, influence, blade_ids, blade_velocity):
    sources = (positions, strengths, cores)
    pair_sums = untile(lax.map(lambda entry: vortex_terms(entry, sources), (tiles(positions), tiles(strengths), tiles(cores))))
    wake_velocity = -inv_four_pi * untile(lax.map(lambda entry: wake_terms(entry, sources), (tiles(panel_centers),)))
    onehot = (blade_ids[None, :] == jnp.arange(BLADES, dtype=jnp.int32)[:, None]).astype(jnp.float32)
    kinematic = jnp.dot(blade_velocity.T, onehot, precision=lax.Precision.HIGHEST)
    onset = jnp.asarray(freestream, jnp.float32)[:, None] + kinematic + wake_velocity
    right_side = -lax.optimization_barrier(jnp.sum(panel_normals * onset, axis=0))
    panel_strengths = relax_factor * right_side
    for turn in range(ITERS - 1):
        image = jnp.dot(influence, panel_strengths, precision=lax.Precision.HIGHEST)
        panel_strengths = panel_strengths + relax_factor * (right_side - image)
    weights = (panel_strengths * panel_areas[0])[None, :]
    panel_sources = (panel_centers, weights, panel_areas)
    panel_sums = untile(lax.map(lambda entry: panel_terms(entry, panel_sources), (tiles(positions),)))
    velocity = jnp.asarray(freestream, jnp.float32)[:, None] - inv_four_pi * pair_sums[:3] + inv_four_pi * panel_sums
    stretching = -inv_four_pi * pair_sums[3:]
    return (velocity, stretching, panel_strengths)
```

```python
import functools
import math

import jax
import jax.numpy as jnp
from jax import lax
from jax.experimental import pallas as pl
from jax.experimental.pallas import tpu as pltpu
from jax.sharding import PartitionSpec as P

ITERS = 4
PASSES = ITERS - 1
RES = 3
UNITS = 4
RING = 3
LANES = 128
MIB = 1024 * 1024

inv_four_pi = 1.0 / (4.0 * math.pi)
relax_factor = 0.5
freestream = (0.0, 0.0, -1.0)


def lane_sums(block):
    ones = jnp.ones((8, block.shape[1]), jnp.float32)
    return lax.dot_general(
        ones,
        block,
        (((1,), (1,)), ((), ())),
        precision=lax.Precision.HIGHEST,
        preferred_element_type=jnp.float32,
    )


def column(row):
    return jnp.transpose(jnp.broadcast_to(row, (row.shape[1], row.shape[1])))


def body(
    nw,
    np_,
    pos_ref,
    str_ref,
    core_ref,
    cen_ref,
    nrm_ref,
    area_ref,
    infl_ref,
    ids_ref,
    blade_ref,
    vel_ref,
    stretch_ref,
    sigma_ref,
    abuf,
    gp,
    pcol,
    tcol,
    part,
    ptab,
    wacc,
    vacc,
    wk,
    vk,
    rhs,
    rhs_col,
    xrow,
    accbuf,
    ybuf,
    ysum,
    yin,
    fin,
    tout,
    tin,
    res_sem,
    ring_sem,
    psend,
    precv,
    rsend,
    rrecv,
    ysend,
    yrecv,
    fsend,
    frecv,
    tsend,
    trecv,
):
    devices = nw * np_
    donors = nw // np_
    w = lax.axis_index("wake")
    p = lax.axis_index("panel")
    me = w * np_ + p
    rows, cols = infl_ref.shape
    own = cen_ref.shape[1]
    grp = accbuf.shape[0]
    unit = grp // UNITS
    groups = rows // grp
    ring = min(RING, groups)
    per_piece = own // grp
    local = pos_ref.shape[1]

    def peer(n):
        return {"wake": n // np_, "panel": n % np_}

    def resident(g):
        return pltpu.make_async_copy(
            infl_ref.at[pl.ds(pl.multiple_of(g * grp, grp), RES * unit), :],
            abuf.at[pl.ds(pl.multiple_of(g * RES * unit, RES * unit), RES * unit), :],
            res_sem.at[g],
        )

    def streamed(t):
        g = t % groups
        slot = t % ring
        return pltpu.make_async_copy(
            infl_ref.at[pl.ds(pl.multiple_of(g * grp + RES * unit, unit), unit), :],
            abuf.at[pl.ds(pl.multiple_of((groups * RES + slot) * unit, unit), unit), :],
            ring_sem.at[slot],
        )

    @pl.loop(0, groups)
    def _(g):
        resident(g).start()

        @pl.when(g < ring)
        def _():
            streamed(g).start()

    barrier = pltpu.get_barrier_semaphore()

    @pl.loop(1, devices)
    def _(off):
        pl.semaphore_signal(
            barrier, inc=1, device_id=peer((me + off) % devices), device_id_type=pl.DeviceIdType.MESH
        )

    mine = jnp.concatenate(
        [pos_ref[...], str_ref[...], core_ref[...], jnp.zeros((1, local), jnp.float32)], axis=0
    )
    part[me] = mine
    pl.semaphore_wait(barrier, devices - 1)

    def particle_copy(src, to):
        return pltpu.make_async_remote_copy(
            src_ref=part.at[src],
            dst_ref=part.at[src],
            send_sem=psend.at[to],
            recv_sem=precv.at[src],
            device_id=peer(to),
            device_id_type=pl.DeviceIdType.MESH,
        )

    @pl.loop(1, devices)
    def _(off):
        particle_copy(me, (me + off) % devices).start()

    for b in range(own // LANES):
        lanes = slice(b * LANES, (b + 1) * LANES)
        for d in range(3):
            pcol[d, lanes, :] = column(cen_ref[d : d + 1, lanes])
        pcol[3, lanes, :] = 4.0 * column(area_ref[0:1, lanes])
    for d in range(3):
        tcol[d] = column(pos_ref[d : d + 1, :])
        tcol[3 + d] = column(str_ref[d : d + 1, :])
    core = core_ref[0:1, :]
    tcol[6] = column(0.5 * core * core)

    @pl.loop(1, devices)
    def _(off):
        src = (me + devices - off) % devices
        particle_copy(src, src).wait_recv()

    @pl.loop(0, devices)
    def _(n):
        blk = part[n]
        px, py, pz = blk[0:1], blk[1:2], blk[2:3]
        sx, sy, sz = blk[3:4], blk[4:5], blk[5:6]
        core = blk[6:7]
        ptab[n, 0:1, :] = core * core
        ptab[n, 1:2, :] = py * sz - pz * sy
        ptab[n, 2:3, :] = pz * sx - px * sz
        ptab[n, 3:4, :] = px * sy - py * sx

    tile = 32

    @pl.loop(0, own // LANES)
    def _(b):
        @pl.loop(0, LANES // tile)
        def _(i):
            first = pl.multiple_of(b * LANES + i * tile, tile)
            here = pl.ds(first, tile)
            cx, cy, cz, ca = pcol[0, here, :], pcol[1, here, :], pcol[2, here, :], pcol[3, here, :]

            def visit(n, sums):
                dx = cx - part[n, 0:1, :]
                dy = cy - part[n, 1:2, :]
                dz = cz - part[n, 2:3, :]
                square = dx * dx + dy * dy + dz * dz
                inv = lax.rsqrt(square + ca)
                gp[n, here, :] = inv * inv * inv
                inv = lax.rsqrt(square + ptab[n, 0:1, :])
                fall = inv * inv * inv
                return (
                    sums[0] + fall * part[n, 3:4, :],
                    sums[1] + fall * part[n, 4:5, :],
                    sums[2] + fall * part[n, 5:6, :],
                    sums[3] + fall * ptab[n, 1:2, :],
                    sums[4] + fall * ptab[n, 2:3, :],
                    sums[5] + fall * ptab[n, 3:4, :],
                )

            zero = jnp.zeros((tile, LANES), jnp.float32)
            sums = lax.fori_loop(0, devices, visit, (zero,) * 6, unroll=4)
            for d in range(6):
                wacc[d, pl.ds(pl.multiple_of(i * tile, tile), tile), :] = sums[d]

        for d in range(6):
            wk[b, d : d + 1, :] = lane_sums(wacc[d])[0:1]

    for b in range(own // LANES):
        lanes = slice(b * LANES, (b + 1) * LANES)
        ids = ids_ref[0:1, lanes]
        cx, cy, cz = cen_ref[0:1, lanes], cen_ref[1:2, lanes], cen_ref[2:3, lanes]
        sx, sy, sz = wk[b, 0:1, :], wk[b, 1:2, :], wk[b, 2:3, :]
        wake = (
            cy * sz - cz * sy - wk[b, 3:4, :],
            cz * sx - cx * sz - wk[b, 4:5, :],
            cx * sy - cy * sx - wk[b, 5:6, :],
        )
        total = jnp.zeros((1, LANES), jnp.float32)
        for d in range(3):
            onset = jnp.full((1, LANES), freestream[d], jnp.float32)
            for blade in range(blade_ref.shape[0]):
                onset = onset + jnp.where(ids == blade, blade_ref[blade, d], 0.0)
            total = total + nrm_ref[d : d + 1, lanes] * (onset - inv_four_pi * wake[d])
        rhs[0:1, lanes] = -total

    holder = w // donors
    slot = w % donors

    def rhs_copy(w2, d, q):
        return pltpu.make_async_remote_copy(
            src_ref=rhs,
            dst_ref=rhs_col.at[d, q],
            send_sem=rsend.at[w2],
            recv_sem=rrecv.at[d, q],
            device_id={"wake": w2, "panel": holder},
            device_id_type=pl.DeviceIdType.MESH,
        )

    @pl.loop(0, nw)
    def _(w2):
        @pl.when(jnp.logical_or(w2 != w, holder != p))
        def _():
            rhs_copy(w2, slot, p).start()

    @pl.when(holder == p)
    def _():
        rhs_col[slot, p] = rhs[...]

    small = 16

    @pl.loop(0, local // small)
    def _(i):
        here = pl.ds(pl.multiple_of(i * small, small), small)
        tx, ty, tz = tcol[0, here, :], tcol[1, here, :], tcol[2, here, :]
        ux, uy, uz = tcol[3, here, :], tcol[4, here, :], tcol[5, here, :]
        tcore = tcol[6, here, :]

        def visit(n, sums):
            dx = tx - part[n, 0:1, :]
            dy = ty - part[n, 1:2, :]
            dz = tz - part[n, 2:3, :]
            inv = lax.rsqrt(dx * dx + dy * dy + dz * dz + (tcore + 0.5 * ptab[n, 0:1, :]))
            inv2 = inv * inv
            fall = inv2 * inv
            along = 3.0 * (fall * inv2) * (ux * dx + uy * dy + uz * dz)
            src = [part[n, 3 + d : 4 + d, :] for d in range(3)]
            src += [ptab[n, 1 + d : 2 + d, :] for d in range(3)]
            return tuple(sums[d] + fall * src[d] for d in range(6)) + tuple(
                sums[6 + d] + along * src[d] for d in range(6)
            )

        zero = jnp.zeros((small, LANES), jnp.float32)
        sums = lax.fori_loop(0, devices, visit, (zero,) * 12, unroll=4)
        for d in range(12):
            vacc[d, here, :] = sums[d]

    for d in range(12):
        vk[d : d + 1, :] = lane_sums(vacc[d])[0:1]

    @pl.loop(0, nw)
    def _(k):
        dw = p * donors + k // np_
        q = k % np_

        @pl.when(jnp.logical_or(dw != w, q != p))
        def _():
            rhs_copy(0, k // np_, q).wait_recv()

    for d in range(donors):
        for q in range(np_):
            at = (d * np_ + q) * own
            xrow[0:1, at : at + own] = relax_factor * rhs_col[d, q]

    def piece_copy(turn, piece, w2, d, q):
        return pltpu.make_async_remote_copy(
            src_ref=ybuf.at[turn, piece],
            dst_ref=yin.at[turn, d, q, piece],
            send_sem=ysend.at[turn, piece, w2],
            recv_sem=yrecv.at[turn, d, q, piece],
            device_id={"wake": w2, "panel": holder},
            device_id_type=pl.DeviceIdType.MESH,
        )

    def final_copy(piece, q):
        return pltpu.make_async_remote_copy(
            src_ref=ysum.at[piece],
            dst_ref=fin.at[q],
            send_sem=fsend.at[piece],
            recv_sem=frecv.at[q],
            device_id={"wake": w, "panel": piece},
            device_id_type=pl.DeviceIdType.MESH,
        )

    for turn in range(PASSES):
        if turn > 0:

            @pl.loop(0, nw)
            def _(k):
                d = k // np_
                q = k % np_

                @pl.when(jnp.logical_or(p * donors + d != w, q != p))
                def _():
                    @pl.loop(0, np_)
                    def _(piece):
                        piece_copy(turn - 1, piece, 0, d, q).wait_recv()

            for d in range(donors):
                for piece in range(np_):
                    at = (d * np_ + piece) * own
                    image = yin[turn - 1, d, 0, piece]
                    for q in range(1, np_):
                        image = image + yin[turn - 1, d, q, piece]
                    xrow[0:1, at : at + own] = xrow[0:1, at : at + own] + relax_factor * (
                        rhs_col[d, piece] - image
                    )

        @pl.loop(0, np_)
        def _(piece):
            @pl.loop(0, per_piece)
            def _(h):
                g = piece * per_piece + h
                t = turn * groups + g
                if turn == 0:
                    resident(g).wait()
                streamed(t).wait()

                @pl.loop(0, UNITS)
                def _(k):
                    at = jnp.where(k < RES, g * RES + k, groups * RES + t % ring)
                    at = pl.multiple_of(at * unit, unit)
                    acc = jnp.zeros((unit, LANES), jnp.float32)
                    for c in range(cols // LANES):
                        lanes = slice(c * LANES, (c + 1) * LANES)
                        acc = acc + abuf[pl.ds(at, unit), lanes] * xrow[0:1, lanes]
                    accbuf[pl.ds(pl.multiple_of(k * unit, unit), unit), :] = acc

                @pl.when(t + ring < PASSES * groups)
                def _():
                    streamed(t + ring).start()

                sums = lane_sums(accbuf[...])[0:1]
                lanes = pl.ds(pl.multiple_of(h * grp, grp), grp)
                if turn == 0:
                    ysum[piece, 0:1, lanes] = sums
                else:
                    ysum[piece, 0:1, lanes] = ysum[piece, 0:1, lanes] + sums
                if turn < PASSES - 1:
                    ybuf[turn, piece, 0:1, lanes] = sums

            if turn < PASSES - 1:

                @pl.loop(0, nw)
                def _(w2):
                    @pl.when(jnp.logical_or(w2 != w, holder != p))
                    def _():
                        piece_copy(turn, piece, w2, slot, p).start()

                @pl.when(holder == p)
                def _():
                    yin[turn, slot, p, piece] = ybuf[turn, piece]
            else:

                @pl.when(piece != p)
                def _():
                    final_copy(piece, p).start()

                @pl.when(piece == p)
                def _():
                    fin[p] = ysum[piece]

    @pl.loop(0, np_)
    def _(q):
        @pl.when(q != p)
        def _():
            final_copy(p, q).wait_recv()

    image = fin[0]
    for q in range(1, np_):
        image = image + fin[q]
    sigma = relax_factor * (ITERS * rhs[...] - image)
    sigma_ref[...] = sigma
    weights = sigma * area_ref[...]
    for b in range(own // LANES):
        lanes = slice(b * LANES, (b + 1) * LANES)
        col = column(weights[:, lanes])
        for d in range(3):
            pcol[d, lanes, :] = col * pcol[d, lanes, :]
        pcol[3, lanes, :] = col

    def sum_copy(n, src):
        return pltpu.make_async_remote_copy(
            src_ref=tout.at[n],
            dst_ref=tin.at[src],
            send_sem=tsend.at[n],
            recv_sem=trecv.at[src],
            device_id=peer(n),
            device_id_type=pl.DeviceIdType.MESH,
        )

    wide = 4

    @pl.loop(0, devices // wide)
    def _(c):
        def visit(i, sums):
            here = pl.ds(pl.multiple_of(i * 8, 8), 8)
            ws = [pcol[d, here, :] for d in (3, 0, 1, 2)]
            fresh = []
            for e in range(wide):
                fall = gp[c * wide + e, here, :]
                for d in range(4):
                    fresh.append(sums[e * 4 + d] + fall * ws[d])
            return tuple(fresh)

        zero = jnp.zeros((8, LANES), jnp.float32)
        sums = lax.fori_loop(0, own // 8, visit, (zero,) * (4 * wide), unroll=4)
        for e in range(wide):
            n = c * wide + e
            for d in range(4):
                tout[n, d : d + 1, :] = jnp.sum(sums[e * 4 + d], axis=0, keepdims=True)

            @pl.when(n != me)
            def _():
                sum_copy(n, me).start()

            @pl.when(n == me)
            def _():
                tin[me] = tout[n]

    @pl.loop(1, devices)
    def _(off):
        src = (me + devices - off) % devices
        sum_copy(src, src).wait_recv()

    pan = lax.fori_loop(1, devices, lambda n, s: s + tin[n], tin[0])
    pos = [pos_ref[d : d + 1, :] for d in range(3)]
    strn = [str_ref[d : d + 1, :] for d in range(3)]
    fs = [vk[d : d + 1, :] for d in range(3)]
    als = [vk[6 + d : 7 + d, :] for d in range(3)]
    for d in range(3):
        e, f = (d + 1) % 3, (d + 2) % 3
        pair = pos[e] * fs[f] - pos[f] * fs[e] - vk[3 + d : 4 + d, :]
        twist = strn[e] * fs[f] - strn[f] * fs[e]
        bend = pos[e] * als[f] - pos[f] * als[e] - vk[9 + d : 10 + d, :]
        panel = pos[d] * pan[0:1] - pan[1 + d : 2 + d]
        vel_ref[d : d + 1, :] = freestream[d] - inv_four_pi * pair + inv_four_pi * panel
        stretch_ref[d : d + 1, :] = -inv_four_pi * (twist - bend)

    @pl.loop(1, devices)
    def _(off):
        n = (me + off) % devices
        particle_copy(me, n).wait_send()
        sum_copy(n, me).wait_send()

    @pl.loop(0, nw)
    def _(w2):
        @pl.when(jnp.logical_or(w2 != w, holder != p))
        def _():
            rhs_copy(w2, slot, p).wait_send()
            for turn in range(PASSES - 1):

                @pl.loop(0, np_)
                def _(piece):
                    piece_copy(turn, piece, w2, slot, p).wait_send()

    @pl.loop(0, np_)
    def _(piece):
        @pl.when(piece != p)
        def _():
            final_copy(piece, p).wait_send()


def per_device(
    nw,
    np_,
    positions,
    strengths,
    cores,
    panel_centers,
    panel_normals,
    panel_areas,
    influence,
    blade_ids,
    blade_velocity,
):
    rows, cols = influence.shape
    own = panel_centers.shape[1]
    local = positions.shape[1]
    devices = nw * np_
    donors = nw // np_
    grp = min(256, own)
    unit = grp // UNITS
    groups = rows // grp
    f32 = jnp.float32
    vmem = pl.BlockSpec(memory_space=pltpu.VMEM)
    dma = pltpu.SemaphoreType.DMA
    velocity, stretching, sigma = pl.pallas_call(
        functools.partial(body, nw, np_),
        out_shape=(
            jax.ShapeDtypeStruct((3, local), f32),
            jax.ShapeDtypeStruct((3, local), f32),
            jax.ShapeDtypeStruct((1, own), f32),
        ),
        in_specs=[vmem] * 6
        + [pl.BlockSpec(memory_space=pl.ANY), vmem, pl.BlockSpec(memory_space=pltpu.SMEM)],
        out_specs=(vmem, vmem, vmem),
        scratch_shapes=[
            pltpu.VMEM(((groups * RES + RING) * unit, cols), f32),
            pltpu.VMEM((devices, own, LANES), f32),
            pltpu.VMEM((4, own, LANES), f32),
            pltpu.VMEM((7, local, LANES), f32),
            pltpu.VMEM((devices, 8, local), f32),
            pltpu.VMEM((devices, 4, local), f32),
            pltpu.VMEM((6, LANES, LANES), f32),
            pltpu.VMEM((12, local, LANES), f32),
            pltpu.VMEM((own // LANES, 8, LANES), f32),
            pltpu.VMEM((16, local), f32),
            pltpu.VMEM((1, own), f32),
            pltpu.VMEM((donors, np_, 1, own), f32),
            pltpu.VMEM((1, cols), f32),
            pltpu.VMEM((grp, LANES), f32),
            pltpu.VMEM((PASSES - 1, np_, 1, own), f32),
            pltpu.VMEM((np_, 1, own), f32),
            pltpu.VMEM((PASSES - 1, donors, np_, np_, 1, own), f32),
            pltpu.VMEM((np_, 1, own), f32),
            pltpu.VMEM((devices, 4, local), f32),
            pltpu.VMEM((devices, 4, local), f32),
            dma((groups,)),
            dma((RING,)),
            dma((devices,)),
            dma((devices,)),
            dma((nw,)),
            dma((donors, np_)),
            dma((PASSES - 1, np_, nw)),
            dma((PASSES - 1, donors, np_, np_)),
            dma((np_,)),
            dma((np_,)),
            dma((devices,)),
            dma((devices,)),
        ],
        compiler_params=pltpu.CompilerParams(
            collective_id=0, has_side_effects=True, vmem_limit_bytes=int(63.9 * MIB)
        ),
        name="rotor",
    )(
        positions,
        strengths,
        cores,
        panel_centers,
        panel_normals,
        panel_areas,
        influence,
        blade_ids.reshape(1, own),
        blade_velocity,
    )
    return velocity, stretching, sigma.reshape(own)


def solution(mesh):
    whole = P(None, ("groups", "wake", "panel"))
    line = P(("groups", "wake", "panel"))
    in_specs = (whole,) * 6 + (P(("groups", "wake"), "panel"), line, P("groups", None))
    return jax.shard_map(
        functools.partial(per_device, mesh.shape["wake"], mesh.shape["panel"]),
        mesh=mesh,
        in_specs=in_specs,
        out_specs=(whole, whole, line),
        check_vma=False,
    )
```

```python
import functools
import math

import jax
import jax.numpy as jnp
from jax import lax
from jax.experimental import pallas as pl
from jax.experimental.pallas import tpu as pltpu
from jax.sharding import PartitionSpec as P

ITERS = 4
PASSES = ITERS - 1
RES = 3
UNITS = 4
RING = 3
LANES = 128
MIB = 1024 * 1024

inv_four_pi = 1.0 / (4.0 * math.pi)
relax_factor = 0.5
freestream = (0.0, 0.0, -1.0)


def lane_sums(block):
    ones = jnp.ones((8, block.shape[1]), jnp.bfloat16)
    total = None
    for _ in range(3):
        term = block.astype(jnp.bfloat16)
        block = block - term.astype(jnp.float32)
        sums = lax.dot_general(
            ones, term, (((1,), (1,)), ((), ())), preferred_element_type=jnp.float32
        )
        total = sums if total is None else total + sums
    return total


def column(row):
    return jnp.transpose(jnp.broadcast_to(row, (row.shape[1], row.shape[1])))


def body(
    nw,
    np_,
    pos_ref,
    str_ref,
    core_ref,
    cen_ref,
    nrm_ref,
    area_ref,
    infl_ref,
    ids_ref,
    blade_ref,
    vel_ref,
    stretch_ref,
    sigma_ref,
    abuf,
    gp,
    pcol,
    tcol,
    part,
    ptab,
    wacc,
    vacc,
    wk,
    vk,
    rhs,
    rhs_col,
    xrow,
    accbuf,
    ybuf,
    ysum,
    yin,
    fin,
    tout,
    tin,
    res_sem,
    ring_sem,
    psend,
    precv,
    rsend,
    rrecv,
    ysend,
    yrecv,
    fsend,
    frecv,
    tsend,
    trecv,
):
    devices = nw * np_
    donors = nw // np_
    w = lax.axis_index("wake")
    p = lax.axis_index("panel")
    me = w * np_ + p
    rows, cols = infl_ref.shape
    own = cen_ref.shape[1]
    grp = min(256, own)
    unit = grp // UNITS
    groups = rows // grp
    ring = min(RING, groups)
    per_piece = own // grp
    local = pos_ref.shape[1]

    def peer(n):
        return {"wake": n // np_, "panel": n % np_}

    def resident(g):
        return pltpu.make_async_copy(
            infl_ref.at[pl.ds(pl.multiple_of(g * grp, grp), RES * unit), :],
            abuf.at[pl.ds(pl.multiple_of(g * RES * unit, RES * unit), RES * unit), :],
            res_sem.at[g],
        )

    def streamed(t):
        g = t % groups
        slot = t % ring
        return pltpu.make_async_copy(
            infl_ref.at[pl.ds(pl.multiple_of(g * grp + RES * unit, unit), unit), :],
            abuf.at[pl.ds(pl.multiple_of((groups * RES + slot) * unit, unit), unit), :],
            ring_sem.at[slot],
        )

    @pl.loop(0, groups)
    def _(g):
        resident(g).start()

        @pl.when(g < ring)
        def _():
            streamed(g).start()

    barrier = pltpu.get_barrier_semaphore()

    @pl.loop(1, devices)
    def _(off):
        pl.semaphore_signal(
            barrier, inc=1, device_id=peer((me + off) % devices), device_id_type=pl.DeviceIdType.MESH
        )

    mine = jnp.concatenate(
        [pos_ref[...], str_ref[...], core_ref[...], jnp.zeros((1, local), jnp.float32)], axis=0
    )
    part[me] = mine
    pl.semaphore_wait(barrier, devices - 1)

    def particle_copy(src, to):
        return pltpu.make_async_remote_copy(
            src_ref=part.at[src],
            dst_ref=part.at[src],
            send_sem=psend.at[to],
            recv_sem=precv.at[src],
            device_id=peer(to),
            device_id_type=pl.DeviceIdType.MESH,
        )

    @pl.loop(1, devices)
    def _(off):
        particle_copy(me, (me + off) % devices).start()

    for b in range(own // LANES):
        lanes = slice(b * LANES, (b + 1) * LANES)
        for d in range(3):
            pcol[d, lanes, :] = column(cen_ref[d : d + 1, lanes])
        pcol[3, lanes, :] = 4.0 * column(area_ref[0:1, lanes])
    for d in range(3):
        tcol[d] = column(pos_ref[d : d + 1, :])
        tcol[3 + d] = column(str_ref[d : d + 1, :])
    core = core_ref[0:1, :]
    tcol[6] = column(0.5 * core * core)

    @pl.loop(1, devices)
    def _(off):
        src = (me + devices - off) % devices
        particle_copy(src, src).wait_recv()

    @pl.loop(0, devices)
    def _(n):
        blk = part[n]
        px, py, pz = blk[0:1], blk[1:2], blk[2:3]
        sx, sy, sz = blk[3:4], blk[4:5], blk[5:6]
        core = blk[6:7]
        ptab[n, 0:1, :] = core * core
        ptab[n, 1:2, :] = py * sz - pz * sy
        ptab[n, 2:3, :] = pz * sx - px * sz
        ptab[n, 3:4, :] = px * sy - py * sx

    tile = 32

    @pl.loop(0, own // LANES)
    def _(b):
        @pl.loop(0, LANES // tile)
        def _(i):
            first = pl.multiple_of(b * LANES + i * tile, tile)
            here = pl.ds(first, tile)
            cx, cy, cz, ca = pcol[0, here, :], pcol[1, here, :], pcol[2, here, :], pcol[3, here, :]

            def visit(n, sums):
                dx = cx - part[n, 0:1, :]
                dy = cy - part[n, 1:2, :]
                dz = cz - part[n, 2:3, :]
                square = dx * dx + dy * dy + dz * dz
                inv = lax.rsqrt(square + ca)
                gp[n, here, :] = inv * inv * inv
                inv = lax.rsqrt(square + ptab[n, 0:1, :])
                fall = inv * inv * inv
                return (
                    sums[0] + fall * part[n, 3:4, :],
                    sums[1] + fall * part[n, 4:5, :],
                    sums[2] + fall * part[n, 5:6, :],
                    sums[3] + fall * ptab[n, 1:2, :],
                    sums[4] + fall * ptab[n, 2:3, :],
                    sums[5] + fall * ptab[n, 3:4, :],
                )

            zero = jnp.zeros((tile, LANES), jnp.float32)
            sums = lax.fori_loop(0, devices, visit, (zero,) * 6, unroll=4)
            for d in range(6):
                wacc[d, pl.ds(pl.multiple_of(i * tile, tile), tile), :] = sums[d]

        for d in range(6):
            wk[b, d : d + 1, :] = lane_sums(wacc[d])[0:1]

    for b in range(own // LANES):
        lanes = slice(b * LANES, (b + 1) * LANES)
        ids = ids_ref[0:1, lanes]
        cx, cy, cz = cen_ref[0:1, lanes], cen_ref[1:2, lanes], cen_ref[2:3, lanes]
        sx, sy, sz = wk[b, 0:1, :], wk[b, 1:2, :], wk[b, 2:3, :]
        wake = (
            cy * sz - cz * sy - wk[b, 3:4, :],
            cz * sx - cx * sz - wk[b, 4:5, :],
            cx * sy - cy * sx - wk[b, 5:6, :],
        )
        total = jnp.zeros((1, LANES), jnp.float32)
        for d in range(3):
            onset = jnp.full((1, LANES), freestream[d], jnp.float32)
            for blade in range(blade_ref.shape[0]):
                onset = onset + jnp.where(ids == blade, blade_ref[blade, d], 0.0)
            total = total + nrm_ref[d : d + 1, lanes] * (onset - inv_four_pi * wake[d])
        rhs[0:1, lanes] = -total

    holder = w // donors
    slot = w % donors

    def rhs_copy(w2, d, q):
        return pltpu.make_async_remote_copy(
            src_ref=rhs,
            dst_ref=rhs_col.at[d, q],
            send_sem=rsend.at[w2],
            recv_sem=rrecv.at[d, q],
            device_id={"wake": w2, "panel": holder},
            device_id_type=pl.DeviceIdType.MESH,
        )

    @pl.loop(0, nw)
    def _(w2):
        @pl.when(jnp.logical_or(w2 != w, holder != p))
        def _():
            rhs_copy(w2, slot, p).start()

    @pl.when(holder == p)
    def _():
        rhs_col[slot, p] = rhs[...]

    small = 16

    @pl.loop(0, local // small)
    def _(i):
        here = pl.ds(pl.multiple_of(i * small, small), small)
        tx, ty, tz = tcol[0, here, :], tcol[1, here, :], tcol[2, here, :]
        ux, uy, uz = tcol[3, here, :], tcol[4, here, :], tcol[5, here, :]
        tcore = tcol[6, here, :]

        def visit(n, sums):
            dx = tx - part[n, 0:1, :]
            dy = ty - part[n, 1:2, :]
            dz = tz - part[n, 2:3, :]
            inv = lax.rsqrt(dx * dx + dy * dy + dz * dz + (tcore + 0.5 * ptab[n, 0:1, :]))
            inv2 = inv * inv
            fall = inv2 * inv
            along = 3.0 * (fall * inv2) * (ux * dx + uy * dy + uz * dz)
            src = [part[n, 3 + d : 4 + d, :] for d in range(3)]
            src += [ptab[n, 1 + d : 2 + d, :] for d in range(3)]
            return tuple(sums[d] + fall * src[d] for d in range(6)) + tuple(
                sums[6 + d] + along * src[d] for d in range(6)
            )

        zero = jnp.zeros((small, LANES), jnp.float32)
        sums = lax.fori_loop(0, devices, visit, (zero,) * 12, unroll=4)
        for d in range(12):
            vacc[d, here, :] = sums[d]

    for d in range(12):
        vk[d : d + 1, :] = lane_sums(vacc[d])[0:1]

    @pl.loop(0, nw)
    def _(k):
        dw = p * donors + k // np_
        q = k % np_

        @pl.when(jnp.logical_or(dw != w, q != p))
        def _():
            rhs_copy(0, k // np_, q).wait_recv()

    for d in range(donors):
        for q in range(np_):
            at = (d * np_ + q) * own
            xrow[0:1, at : at + own] = relax_factor * rhs_col[d, q]

    def piece_copy(turn, piece, w2, d, q):
        return pltpu.make_async_remote_copy(
            src_ref=ybuf.at[turn, piece],
            dst_ref=yin.at[turn, d, q, piece],
            send_sem=ysend.at[turn, piece, w2],
            recv_sem=yrecv.at[turn, d, q, piece],
            device_id={"wake": w2, "panel": holder},
            device_id_type=pl.DeviceIdType.MESH,
        )

    def final_copy(piece, q):
        return pltpu.make_async_remote_copy(
            src_ref=ysum.at[piece],
            dst_ref=fin.at[q],
            send_sem=fsend.at[piece],
            recv_sem=frecv.at[q],
            device_id={"wake": w, "panel": piece},
            device_id_type=pl.DeviceIdType.MESH,
        )

    for turn in range(PASSES):
        if turn > 0:

            @pl.loop(0, nw)
            def _(k):
                d = k // np_
                q = k % np_

                @pl.when(jnp.logical_or(p * donors + d != w, q != p))
                def _():
                    @pl.loop(0, np_)
                    def _(piece):
                        piece_copy(turn - 1, piece, 0, d, q).wait_recv()

            for d in range(donors):
                for piece in range(np_):
                    at = (d * np_ + piece) * own
                    image = yin[turn - 1, d, 0, piece]
                    for q in range(1, np_):
                        image = image + yin[turn - 1, d, q, piece]
                    xrow[0:1, at : at + own] = xrow[0:1, at : at + own] + relax_factor * (
                        rhs_col[d, piece] - image
                    )

        @pl.loop(0, np_)
        def _(piece):
            @pl.loop(0, per_piece)
            def _(h):
                g = piece * per_piece + h
                t = turn * groups + g
                if turn == 0:
                    resident(g).wait()
                streamed(t).wait()

                @pl.loop(0, UNITS)
                def _(k):
                    at = jnp.where(k < RES, g * RES + k, groups * RES + t % ring)
                    at = pl.multiple_of(at * unit, unit)
                    acc = jnp.zeros((unit, LANES), jnp.float32)
                    for c in range(cols // LANES):
                        lanes = slice(c * LANES, (c + 1) * LANES)
                        acc = acc + abuf[pl.ds(at, unit), lanes] * xrow[0:1, lanes]
                    accbuf[pl.ds(pl.multiple_of(h * grp + k * unit, unit), unit), :] = acc

                @pl.when(t + ring < PASSES * groups)
                def _():
                    streamed(t + ring).start()

            for at in range(0, own, grp):
                sums = lane_sums(accbuf[at : at + grp, :])[0:1]
                lanes = slice(at, at + grp)
                if turn == 0:
                    ysum[piece, 0:1, lanes] = sums
                else:
                    ysum[piece, 0:1, lanes] = ysum[piece, 0:1, lanes] + sums
                if turn < PASSES - 1:
                    ybuf[turn, piece, 0:1, lanes] = sums

            if turn < PASSES - 1:

                @pl.loop(0, nw)
                def _(w2):
                    @pl.when(jnp.logical_or(w2 != w, holder != p))
                    def _():
                        piece_copy(turn, piece, w2, slot, p).start()

                @pl.when(holder == p)
                def _():
                    yin[turn, slot, p, piece] = ybuf[turn, piece]
            else:

                @pl.when(piece != p)
                def _():
                    final_copy(piece, p).start()

                @pl.when(piece == p)
                def _():
                    fin[p] = ysum[piece]

    @pl.loop(0, np_)
    def _(q):
        @pl.when(q != p)
        def _():
            final_copy(p, q).wait_recv()

    image = fin[0]
    for q in range(1, np_):
        image = image + fin[q]
    sigma = relax_factor * (ITERS * rhs[...] - image)
    sigma_ref[...] = sigma
    weights = sigma * area_ref[...]
    for b in range(own // LANES):
        lanes = slice(b * LANES, (b + 1) * LANES)
        col = column(weights[:, lanes])
        for d in range(3):
            pcol[d, lanes, :] = col * pcol[d, lanes, :]
        pcol[3, lanes, :] = col

    def sum_copy(n, src):
        return pltpu.make_async_remote_copy(
            src_ref=tout.at[n],
            dst_ref=tin.at[src],
            send_sem=tsend.at[n],
            recv_sem=trecv.at[src],
            device_id=peer(n),
            device_id_type=pl.DeviceIdType.MESH,
        )

    wide = 4

    @pl.loop(0, devices // wide)
    def _(c):
        def visit(i, sums):
            here = pl.ds(pl.multiple_of(i * 8, 8), 8)
            ws = [pcol[d, here, :] for d in (3, 0, 1, 2)]
            fresh = []
            for e in range(wide):
                fall = gp[c * wide + e, here, :]
                for d in range(4):
                    fresh.append(sums[e * 4 + d] + fall * ws[d])
            return tuple(fresh)

        zero = jnp.zeros((8, LANES), jnp.float32)
        sums = lax.fori_loop(0, own // 8, visit, (zero,) * (4 * wide), unroll=4)
        for e in range(wide):
            n = c * wide + e
            for d in range(4):
                tout[n, d : d + 1, :] = jnp.sum(sums[e * 4 + d], axis=0, keepdims=True)

            @pl.when(n != me)
            def _():
                sum_copy(n, me).start()

            @pl.when(n == me)
            def _():
                tin[me] = tout[n]

    @pl.loop(1, devices)
    def _(off):
        src = (me + devices - off) % devices
        sum_copy(src, src).wait_recv()

    pan = lax.fori_loop(1, devices, lambda n, s: s + tin[n], tin[0])
    pos = [pos_ref[d : d + 1, :] for d in range(3)]
    strn = [str_ref[d : d + 1, :] for d in range(3)]
    fs = [vk[d : d + 1, :] for d in range(3)]
    als = [vk[6 + d : 7 + d, :] for d in range(3)]
    for d in range(3):
        e, f = (d + 1) % 3, (d + 2) % 3
        pair = pos[e] * fs[f] - pos[f] * fs[e] - vk[3 + d : 4 + d, :]
        twist = strn[e] * fs[f] - strn[f] * fs[e]
        bend = pos[e] * als[f] - pos[f] * als[e] - vk[9 + d : 10 + d, :]
        panel = pos[d] * pan[0:1] - pan[1 + d : 2 + d]
        vel_ref[d : d + 1, :] = freestream[d] - inv_four_pi * pair + inv_four_pi * panel
        stretch_ref[d : d + 1, :] = -inv_four_pi * (twist - bend)

    @pl.loop(1, devices)
    def _(off):
        n = (me + off) % devices
        particle_copy(me, n).wait_send()
        sum_copy(n, me).wait_send()

    @pl.loop(0, nw)
    def _(w2):
        @pl.when(jnp.logical_or(w2 != w, holder != p))
        def _():
            rhs_copy(w2, slot, p).wait_send()
            for turn in range(PASSES - 1):

                @pl.loop(0, np_)
                def _(piece):
                    piece_copy(turn, piece, w2, slot, p).wait_send()

    @pl.loop(0, np_)
    def _(piece):
        @pl.when(piece != p)
        def _():
            final_copy(piece, p).wait_send()


def per_device(
    nw,
    np_,
    positions,
    strengths,
    cores,
    panel_centers,
    panel_normals,
    panel_areas,
    influence,
    blade_ids,
    blade_velocity,
):
    rows, cols = influence.shape
    own = panel_centers.shape[1]
    local = positions.shape[1]
    devices = nw * np_
    donors = nw // np_
    grp = min(256, own)
    unit = grp // UNITS
    groups = rows // grp
    f32 = jnp.float32
    vmem = pl.BlockSpec(memory_space=pltpu.VMEM)
    dma = pltpu.SemaphoreType.DMA
    velocity, stretching, sigma = pl.pallas_call(
        functools.partial(body, nw, np_),
        out_shape=(
            jax.ShapeDtypeStruct((3, local), f32),
            jax.ShapeDtypeStruct((3, local), f32),
            jax.ShapeDtypeStruct((1, own), f32),
        ),
        in_specs=[vmem] * 6
        + [pl.BlockSpec(memory_space=pl.ANY), vmem, pl.BlockSpec(memory_space=pltpu.SMEM)],
        out_specs=(vmem, vmem, vmem),
        scratch_shapes=[
            pltpu.VMEM(((groups * RES + RING) * unit, cols), f32),
            pltpu.VMEM((devices, own, LANES), f32),
            pltpu.VMEM((4, own, LANES), f32),
            pltpu.VMEM((7, local, LANES), f32),
            pltpu.VMEM((devices, 8, local), f32),
            pltpu.VMEM((devices, 4, local), f32),
            pltpu.VMEM((6, LANES, LANES), f32),
            pltpu.VMEM((12, local, LANES), f32),
            pltpu.VMEM((own // LANES, 8, LANES), f32),
            pltpu.VMEM((16, local), f32),
            pltpu.VMEM((1, own), f32),
            pltpu.VMEM((donors, np_, 1, own), f32),
            pltpu.VMEM((1, cols), f32),
            pltpu.VMEM((own, LANES), f32),
            pltpu.VMEM((PASSES - 1, np_, 1, own), f32),
            pltpu.VMEM((np_, 1, own), f32),
            pltpu.VMEM((PASSES - 1, donors, np_, np_, 1, own), f32),
            pltpu.VMEM((np_, 1, own), f32),
            pltpu.VMEM((devices, 4, local), f32),
            pltpu.VMEM((devices, 4, local), f32),
            dma((groups,)),
            dma((RING,)),
            dma((devices,)),
            dma((devices,)),
            dma((nw,)),
            dma((donors, np_)),
            dma((PASSES - 1, np_, nw)),
            dma((PASSES - 1, donors, np_, np_)),
            dma((np_,)),
            dma((np_,)),
            dma((devices,)),
            dma((devices,)),
        ],
        compiler_params=pltpu.CompilerParams(
            collective_id=0, has_side_effects=True, vmem_limit_bytes=int(63.9 * MIB)
        ),
        name="rotor",
    )(
        positions,
        strengths,
        cores,
        panel_centers,
        panel_normals,
        panel_areas,
        influence,
        blade_ids.reshape(1, own),
        blade_velocity,
    )
    return velocity, stretching, sigma.reshape(own)


def solution(mesh):
    whole = P(None, ("groups", "wake", "panel"))
    line = P(("groups", "wake", "panel"))
    in_specs = (whole,) * 6 + (P(("groups", "wake"), "panel"), line, P("groups", None))
    return jax.shard_map(
        functools.partial(per_device, mesh.shape["wake"], mesh.shape["panel"]),
        mesh=mesh,
        in_specs=in_specs,
        out_specs=(whole, whole, line),
        check_vma=False,
    )
```
